256 devices in a mesh: lon: 32 (over z, y_hi, core), lat: 8 (over y_lo, x).
Axes of the slice: x: 4, y: 4 (y_hi: 2, y_lo: 2; y = y_hi * 2 + y_lo), z: 8, core: 2. Of those that a mesh axis runs over, the one named last changes fastest.
Arguments:
- zonal_current: float32 [48, 512, 4096], P(None, 'lat', 'lon'), may hold values from -6 to 6
- meridional_current: float32 [48, 512, 4096], P(None, 'lat', 'lon'), may hold values from -6 to 6
- heat_anomaly: float32 [48, 512, 4096], P(None, 'lat', 'lon'), may hold values from -6 to 6
- saltiness_anomaly: float32 [48, 512, 4096], P(None, 'lat', 'lon'), may hold values from -6 to 6
- submerged_strata_number: int32 [512, 4096], P('lat', 'lon'), may hold values from 0 to 48
Outputs:
- next_zonal_current: float32 [48, 512, 4096], P(None, 'lat', 'lon')
- next_meridional_current: float32 [48, 512, 4096], P(None, 'lat', 'lon')
- next_heat_anomaly: float32 [48, 512, 4096], P(None, 'lat', 'lon')
- next_saltiness: float32 [48, 512, 4096], P(None, 'lat', 'lon')
The draws below stay inside these ranges and needn't reach their ends.
All inputs are finite; a program needn't handle non-finite values.
Results may differ from the reference program's by a relative error of at most 0.0003.
Values sent between devices are 32-bit elements; how exact they have to be, the bound alone decides.
No kernel may reach another device: no remote copies, remote signals or barrier semaphores. Data moves between devices by JAX's collectives and lax.ppermute only.
A program may use at most 128 MiB of HBM per device.

```python
import math
import jax
import jax.numpy as jnp
from jax import lax

VERTICAL_STRATA = 48
MERIDIAN_POINTS = 512
ZONAL_POINTS = 4096


def set_ends(values, key, least, largest):
    spot = [jax.random.randint(jax.random.fold_in(key, axis), (), 0, length) for axis, length in enumerate(values.shape)]
    main_axis = values.shape.index(max(values.shape))
    next_to = spot[:main_axis] + [(spot[main_axis] + 1) % values.shape[main_axis]] + spot[main_axis + 1:]
    return values.at[tuple(spot)].set(least).at[tuple(next_to)].set(largest)


def level_of(rng, extent, split, smallest, top_value):
    level, own = 1.0, jax.random.fold_in(rng, 6)
    for position, parts in split:
        heights = jnp.exp(jax.random.uniform(jax.random.fold_in(own, position), (parts,), jnp.float32, smallest / len(split), top_value / len(split)))
        level = level * jnp.repeat(heights, extent[position] // parts).reshape([-1 if axis == position else 1 for axis in range(len(extent))])
    return level


def gaussian(key, shape, spread, most, cuts=(), held_as=jnp.bfloat16):
    loudness = level_of(key, shape, cuts, -0.22, 0.18) if cuts else 1.0
    entries = jax.random.normal(key, shape, jnp.float32) * spread * loudness
    return jnp.minimum(jnp.maximum(entries, -most), most).astype(held_as)


def setup_inputs(seed: int = 0) -> dict:
    keys = jax.random.split(jax.random.key(seed), 6)
    zonal_current = gaussian(keys[0], (VERTICAL_STRATA, MERIDIAN_POINTS, ZONAL_POINTS), 1.0, 6.0, ((1, 8), (2, 32)), jnp.float32)
    meridional_current = gaussian(keys[1], (VERTICAL_STRATA, MERIDIAN_POINTS, ZONAL_POINTS), 1.0, 6.0, ((1, 8), (2, 32)), jnp.float32)
    heat_anomaly = gaussian(keys[2], (VERTICAL_STRATA, MERIDIAN_POINTS, ZONAL_POINTS), 1.0, 6.0, ((1, 8), (2, 32)), jnp.float32)
    saltiness_anomaly = gaussian(keys[3], (VERTICAL_STRATA, MERIDIAN_POINTS, ZONAL_POINTS), 1.0, 6.0, ((1, 8), (2, 32)), jnp.float32)
    submerged_strata_number = set_ends(jax.random.randint(keys[4], (MERIDIAN_POINTS, ZONAL_POINTS), 0, VERTICAL_STRATA + 1), jax.random.fold_in(keys[4], 1), 0, VERTICAL_STRATA).astype(jnp.int32)
    return {"zonal_current": zonal_current, "meridional_current": meridional_current, "heat_anomaly": heat_anomaly, "saltiness_anomaly": saltiness_anomaly, "submerged_strata_number": submerged_strata_number}


time_step = 0.1


def centre(values):
    return values[..., 1:-1, 1:-1]


def to_east(values):
    return values[..., 1:-1, 2:]


def to_west(values):
    return values[..., 1:-1, :-2]


def to_north(values):
    return values[..., 2:, 1:-1]


def to_south(values):
    return values[..., :-2, 1:-1]


def column_geometry(stratum_positions):
    layer_number = jnp.arange(stratum_positions).astype(jnp.float32)
    stratum_span = 1.0 + layer_number / stratum_positions
    stratum_centre_height = jnp.cumsum(stratum_span) - 0.5 * stratum_span
    return stratum_span[:, None, None], stratum_centre_height[:, None, None]


def weight_of_water_above(temp_vals, salt_vals, seawater_indicator, stratum_span, stratum_centre_height):
    density = seawater_indicator * (-0.6 * temp_vals - 0.1 * temp_vals * temp_vals + 0.8 * salt_vals + 0.03 * stratum_centre_height * temp_vals)
    weight = density * stratum_span
    return jnp.cumsum(weight, axis=0) - 0.5 * weight


def latitude_terms(first_row, parallels_in_block, total_rows):
    row_index = (first_row + jnp.arange(parallels_in_block)).astype(jnp.float32)
    latitude = (-75.0 + 150.0 * (row_index + 0.5) / total_rows) * (math.pi / 180.0)
    return (1.0 / jnp.cos(latitude))[:, None], (1.5 * jnp.sin(latitude))[:, None]


def advance(zonal_ext, merid_ext, temp_ext, salt_ext, press_ext, wet_ext, inv_dx, coriolis):
    seawater_indicator = centre(wet_ext)
    wet_east = seawater_indicator * to_east(wet_ext)
    wet_west = seawater_indicator * to_west(wet_ext)
    wet_north = seawater_indicator * to_north(wet_ext)
    wet_south = seawater_indicator * to_south(wet_ext)
    zonal_mid = centre(zonal_ext)
    merid_mid = centre(merid_ext)
    flow_east = wet_east * 0.5 * (zonal_mid + to_east(zonal_ext))
    flow_west = wet_west * 0.5 * (zonal_mid + to_west(zonal_ext))
    flow_north = wet_north * 0.5 * (merid_mid + to_north(merid_ext))
    flow_south = wet_south * 0.5 * (merid_mid + to_south(merid_ext))

    def divergence(values):
        middle = centre(values)
        zonal_flux = flow_east * 0.5 * (middle + to_east(values)) - flow_west * 0.5 * (middle + to_west(values))
        merid_flux = flow_north * 0.5 * (middle + to_north(values)) - flow_south * 0.5 * (middle + to_south(values))
        return zonal_flux * inv_dx + merid_flux

    slope_x = wet_east * wet_west * (to_east(press_ext) - to_west(press_ext)) * 0.5 * inv_dx
    slope_y = wet_north * wet_south * (to_north(press_ext) - to_south(press_ext)) * 0.5
    zonal_new = seawater_indicator * (zonal_mid + time_step * (coriolis * merid_mid - slope_x - divergence(zonal_ext)))
    merid_new = seawater_indicator * (merid_mid + time_step * (-coriolis * zonal_mid - slope_y - divergence(merid_ext)))
    temp_new = seawater_indicator * (centre(temp_ext) - time_step * divergence(temp_ext))
    salt_new = seawater_indicator * (centre(salt_ext) - time_step * divergence(salt_ext))
    return zonal_new, merid_new, temp_new, salt_new


def border_extend_block(values, fold_sign):
    wrapped = jnp.concatenate([values[..., -1:], values, values[..., :1]], axis=-1)
    mirrored = fold_sign * jnp.flip(wrapped[..., -1:, :], axis=-1)
    bottom = jnp.zeros_like(wrapped[..., :1, :])
    return jnp.concatenate([bottom, wrapped, mirrored], axis=-2)


def reference(zonal_current, meridional_current, heat_anomaly, saltiness_anomaly, submerged_strata_number):
    stratum_span, stratum_centre_height = column_geometry(VERTICAL_STRATA)
    kmt_float = submerged_strata_number.astype(jnp.float32)
    layer_index = jnp.arange(VERTICAL_STRATA).astype(jnp.float32)[:, None, None]
    seawater_indicator = (layer_index < kmt_float[None]).astype(jnp.float32)
    force_per_area_field = weight_of_water_above(heat_anomaly, saltiness_anomaly, seawater_indicator, stratum_span, stratum_centre_height)
    inv_dx, coriolis = latitude_terms(0, MERIDIAN_POINTS, MERIDIAN_POINTS)
    kmt_ext = border_extend_block(kmt_float, 1.0)

    def advance_one_stratum(level_index):
        def one_stratum_plane(values):
            return lax.dynamic_index_in_dim(values, level_index, 0, keepdims=True)

        wet_ext = (level_index.astype(jnp.float32) < kmt_ext[None]).astype(jnp.float32)
        results = advance(border_extend_block(one_stratum_plane(zonal_current), -1.0), border_extend_block(one_stratum_plane(meridional_current), -1.0),
                          border_extend_block(one_stratum_plane(heat_anomaly), 1.0), border_extend_block(one_stratum_plane(saltiness_anomaly), 1.0),
                          border_extend_block(one_stratum_plane(force_per_area_field), 1.0), wet_ext, inv_dx, coriolis)
        return tuple(result[0] for result in results)

    next_zonal_current, next_meridional_current, next_heat_anomaly, next_saltiness = lax.map(advance_one_stratum, jnp.arange(VERTICAL_STRATA).astype(jnp.int32))
    return (next_zonal_current, next_meridional_current, next_heat_anomaly, next_saltiness)
```

```python
import math

import jax
import jax.numpy as jnp
from jax import lax
from jax.experimental import pallas as pl
from jax.experimental.pallas import tpu as pltpu
from jax.sharding import PartitionSpec as P

NK, NJ, NI = 48, 64, 128
JT = NJ // 8
NQ = NK // 3
CH = 4
CK = NK // CH
F32 = jnp.float32
VM = pl.BlockSpec(memory_space=pltpu.VMEM)
ANY = pl.BlockSpec(memory_space=pl.ANY)
LIMIT = 48 * 1024 * 1024


def lanes():
    return lax.broadcasted_iota(jnp.int32, (8, NI), 1)


def subs():
    return lax.broadcasted_iota(jnp.int32, (8, NI), 0)


def roll(x, shift, axis):
    return pltpu.roll(x, shift, axis)


def place(k, jt):
    return pl.ds(pl.multiple_of(k * NJ, NJ) + 8 * jt, 8)


def tile(ref, k, jt):
    return ref[place(k, jt), :]


def split_pairs(a, b, even):
    return jnp.where(even, a, roll(b, 1, 1)), jnp.where(even, roll(a, 127, 1), b)


def join_pairs(e, w, even):
    return jnp.where(even, e, roll(w, 1, 1)), jnp.where(even, roll(e, 127, 1), w)


def level_terms(k):
    h = 1.0 + k * (1.0 / NK)
    z = (k + 1.0) + k * (k + 1.0) * (0.5 / NK) - 0.5 * h
    return 0.5 * h * (-0.6 + 0.03 * z), -0.05 * h, 0.4 * h


def packed_latitude():
    row = lax.axis_index("lat") * NJ + (lanes() & 7) * 8 + subs()
    total = NJ * lax.axis_size("lat")
    phi = (-75.0 + 150.0 * (row.astype(F32) + 0.5) / total) * (math.pi / 180.0)
    return 1.0 / jnp.cos(phi), 1.5 * jnp.sin(phi)


def pack_kernel(kmt, u, v, t, s, uo, vo, to, so, near, far, ra, rb, sem):
    copies = [
        [
            pltpu.make_async_copy(
                src.at[pl.ds(c * CK * NJ, CK * NJ)],
                dst.at[pl.ds(c * CK * NJ, CK * NJ)],
                sem.at[c, f],
            )
            for f, (src, dst) in enumerate(((u, uo), (v, vo), (t, to), (s, so)))
        ]
        for c in range(CH)
    ]
    for group in copies:
        for copy in group:
            copy.start()
    lon, lat = lax.axis_index("lon"), lax.axis_index("lat")
    lon_even, lat_even = lon % 2 == 0, lat % 2 == 0
    lane = lanes()
    even = (lane & 1) == 0
    spot = [(lane >> 1) == 60 + jh for jh in range(4)]
    outs = (uo, vo, to, so)

    def put(acc, tiles):
        for jh in range(4):
            acc = jnp.where(spot[jh], roll(tiles[jh], 121 + 2 * jh, 1), acc)
        return acc

    kf = [kmt[8 * jt : 8 * jt + 8, :].astype(F32) for jt in range(JT)]
    inner = [
        jnp.minimum(x, jnp.where(lane == 0, roll(x, 127, 1), roll(x, 1, 1))) for x in kf
    ]
    zero = jnp.zeros((8, NI), F32)
    for at, tiles in ((96, kf), (104, inner)):
        e, w = split_pairs(put(zero, tiles[0::2]), put(zero, tiles[1::2]), even)
        for shift in (8, 16, 32, 64):
            e = e + roll(e, shift, 1)
            w = w + roll(w, shift, 1)
        near[at : at + 8, :] = jnp.where(lon_even, e, w)
        far[at : at + 8, :] = jnp.where(lon_even, w, e)

    def step(q, carry):
        new = []
        for f in range(4):
            for i in range(3):
                k = q * 3 + i
                for half in range(2):
                    acc = roll(carry[f * 6 + i * 2 + half], 120, 1)
                    tiles = [tile(outs[f], k, jt) for jt in range(half, JT, 2)]
                    new.append(put(acc, tiles))
        return tuple(new)

    carry = (zero,) * 24
    for c in range(CH):
        for copy in copies[c]:
            copy.wait()
        carry = lax.fori_loop(c * NQ // CH, (c + 1) * NQ // CH, step, carry)
    for f in range(4):
        for i in range(3):
            e, w = split_pairs(carry[f * 6 + i * 2], carry[f * 6 + i * 2 + 1], even)
            at = (f * 3 + i) * 8
            near[at : at + 8, :] = jnp.where(lon_even, e, w)
            far[at : at + 8, :] = jnp.where(lon_even, w, e)

    fold = lat == lax.axis_size("lat") - 1
    order = jnp.where(fold, 127 - lane, lane)
    tops, bottoms = [], []
    for ref in outs:
        top = ref[pl.ds(NJ - 1, NK, stride=NJ), :]
        bottom = ref[pl.ds(0, NK, stride=NJ), :]
        for b in range(6):
            tops.append(top[8 * b : 8 * b + 8, :])
            bottoms.append(bottom[8 * b : 8 * b + 8, :])
    tops.append(jnp.broadcast_to(kf[JT - 1][7:8, :], (8, NI)))
    bottoms.append(jnp.broadcast_to(kf[0][0:1, :], (8, NI)))
    for n, (top, bottom) in enumerate(zip(tops, bottoms)):
        ra[8 * n : 8 * n + 8, :] = jnp.where(lat_even, top, bottom)
        rb[8 * n : 8 * n + 8, :] = jnp.take_along_axis(
            jnp.where(lat_even, bottom, top), order, axis=1, mode="promise_in_bounds"
        )


def main_kernel(
    kmt, u_ref, v_ref, t_ref, s_ref, ou, ov, ot, os, pin, p62, p1, ks, ke, kn, kew, kns, rs, fs
):
    kf = kmt[...].astype(F32)
    lane64 = lax.broadcasted_iota(jnp.int32, (NJ, NI), 1)
    row64 = lax.broadcasted_iota(jnp.int32, (NJ, NI), 0)
    k_e = jnp.minimum(kf, roll(kf, 127, 1))
    k_w = roll(kf, 1, 1)
    k_n = jnp.minimum(kf, roll(kf, NJ - 1, 0))
    k_s = roll(kf, 1, 0)
    ks[...] = kf
    ke[...] = jnp.where(lane64 == NI - 1, 0.0, k_e)
    kew[...] = jnp.where((lane64 == 0) | (lane64 == NI - 1), 0.0, jnp.minimum(k_e, k_w))
    kn[...] = jnp.where(row64 == NJ - 1, 0.0, k_n)
    kns[...] = jnp.where((row64 == 0) | (row64 == NJ - 1), 0.0, jnp.minimum(k_n, k_s))
    r, f = packed_latitude()
    for jt in range(JT):
        rs[8 * jt : 8 * jt + 8, :] = jnp.broadcast_to(0.025 * r[:, jt : jt + 1], (8, NI))
        fs[8 * jt : 8 * jt + 8, :] = jnp.broadcast_to(0.1 * f[:, jt : jt + 1], (8, NI))

    lane, row = lanes(), subs()
    first, row0, row7 = lane == 0, row == 0, row == 7
    even = (lane & 1) == 0
    spot = [(lane >> 1) == 60 + jh for jh in range(4)]
    zero = jnp.zeros((8, NI), F32)

    def fixed(ref, jt):
        return ref[8 * jt : 8 * jt + 8, :]

    def north(now, after):
        return roll(jnp.where(row0, after, now), 7, 0)

    def south(now, before):
        return roll(jnp.where(row7, before, now), 1, 0)

    def level(k, acc, edge):
        kk = k.astype(F32)
        c1, c2, c3 = level_terms(kk)
        press, acc_new = [], []
        for jt in range(JT):
            t = tile(t_ref, k, jt)
            w = t * (c1 + c2 * t) + c3 * tile(s_ref, k, jt)
            w = jnp.where(fixed(ks, jt) > kk, w, 0.0)
            p = acc[jt] + w
            press.append(p)
            acc_new.append(p + w)
        p62[pl.ds(k, 1), :] = press[JT - 1][6:7, :]
        p1[pl.ds(k, 1), :] = press[0][1:2, :]
        edge = [roll(x, 120, 1) for x in edge]
        before = [zero] * 4
        for jt in range(JT):
            q = [tile(ref, k, jt) for ref in (u_ref, v_ref, t_ref, s_ref)]
            up = min(jt + 1, JT - 1)
            r25, f01 = fixed(rs, jt), fixed(fs, jt)
            qe = [x + roll(x, 127, 1) for x in q]
            flow = jnp.where(fixed(ke, jt) > kk, r25, 0.0) * qe[0]
            fe = [flow * x for x in qe]
            qn = [
                x + north(x, tile(ref, k, up)) for x, ref in zip(q, (u_ref, v_ref, t_ref, s_ref))
            ]
            flow = jnp.where(fixed(kn, jt) > kk, 0.025, 0.0) * qn[1]
            fn = [flow * x for x in qn]
            out = [
                x - (a - roll(a, 1, 1)) - (b - south(b, c))
                for x, a, b, c in zip(q, fe, fn, before)
            ]
            before = fn
            p = press[jt]
            pe, pw = roll(p, 127, 1), roll(p, 1, 1)
            spot_p = roll(jnp.where(first, pe, pw), 121 + 2 * (jt // 2), 1)
            edge[jt % 2] = jnp.where(spot[jt // 2], spot_p, edge[jt % 2])
            slope = jnp.where(fixed(kew, jt) > kk, 2.0 * r25, 0.0) * (pe - pw)
            out[0] = out[0] + (f01 * q[1] - slope)
            pn, ps = north(p, press[up]), south(p, press[max(jt - 1, 0)])
            slope = jnp.where(fixed(kns, jt) > kk, 0.05, 0.0) * (pn - ps)
            out[1] = out[1] - (f01 * q[0] + slope)
            wet = fixed(ks, jt) > kk
            for ref, x in zip((ou, ov, ot, os), out):
                ref[place(k, jt), :] = jnp.where(wet, x, 0.0)
        return acc_new, edge

    def step(q, carry):
        acc = list(carry[:JT])
        edges = list(carry[JT:])
        for i in range(3):
            acc, edges[2 * i : 2 * i + 2] = level(q * 3 + i, acc, edges[2 * i : 2 * i + 2])
        return tuple(acc) + tuple(edges)

    carry = lax.fori_loop(0, NQ, step, (zero,) * (JT + 6))
    for i in range(3):
        e, w = split_pairs(carry[JT + 2 * i], carry[JT + 2 * i + 1], even)
        pin[8 * i : 8 * i + 8, :] = e
        pin[24 + 8 * i : 32 + 8 * i, :] = w


def fix_kernel(
    kmt, u_ref, v_ref, t_ref, s_ref, bu, bv, bt, bs, pin, p62, p1,
    near, far, near_in, far_in, ra_in, rb_in, ou, ov, ot, os, buf, rows, sem,
):
    lon, lat = lax.axis_index("lon"), lax.axis_index("lat")
    lon_even, lat_even = lon % 2 == 0, lat % 2 == 0
    is_top, is_bottom = lat == lax.axis_size("lat") - 1, lat == 0
    lane, row = lanes(), subs()
    even = (lane & 1) == 0
    fields = (u_ref, v_ref, t_ref, s_ref)

    level48 = lax.broadcasted_iota(jnp.int32, (NK, NI), 0).astype(F32)
    row48 = lax.broadcasted_iota(jnp.int32, (NK, NI), 0)
    c1, c2, c3 = level_terms(level48)
    sign = jnp.where(is_top, -1.0, 1.0)
    for side in range(2):
        own_row, next_row = (NJ - 1, NJ - 2) if side == 0 else (0, 1)
        use_a = lat_even if side == 0 else jnp.logical_not(lat_even)
        halo = [
            jnp.where(use_a, ra_in[NK * f : NK * f + NK, :], rb_in[NK * f : NK * f + NK, :])
            for f in range(4)
        ]
        k_halo = jnp.where(use_a, ra_in[4 * NK : 4 * NK + 1, :], rb_in[4 * NK : 4 * NK + 1, :])
        if side == 0:
            halo[0], halo[1] = halo[0] * sign, halo[1] * sign
        else:
            k_halo = jnp.where(is_bottom, 0.0, k_halo)
        own = [
            ref[pl.ds(own_row, NK, stride=NJ), :] for ref in fields
        ]
        k_own = kmt[own_row : own_row + 1, :].astype(F32)
        k_next = kmt[next_row : next_row + 1, :].astype(F32)
        k_face = jnp.minimum(k_own, k_halo)
        w = halo[2] * (c1 + c2 * halo[2]) + c3 * halo[3]
        w = jnp.where(level48 < k_halo, w, 0.0)
        total = w + w
        shift = 1
        while shift < NK:
            total = total + jnp.where(row48 >= shift, roll(total, shift, 0), 0.0)
            shift *= 2
        press = total - w
        flow = jnp.where(level48 < k_face, 0.025, 0.0) * (own[1] + halo[1])
        if side == 0:
            flow = -flow
        slope = press - p62[...] if side == 0 else p1[...] - press
        slope = jnp.where(level48 < jnp.minimum(k_face, k_next), 0.05, 0.0) * slope
        for f in range(4):
            add = flow * (own[f] + halo[f])
            if f == 1:
                add = add - slope
            rows[side, f, :, :] = add

    r, _ = packed_latitude()
    r25 = 0.025 * r
    level_of = [((lane >> 3) * 3 + i).astype(F32) for i in range(3)]
    terms = [level_terms(x) for x in level_of]
    sides = []
    for side in range(2):
        use_near = lon_even if side == 0 else jnp.logical_not(lon_even)

        def block(a, b, at):
            return jnp.where(use_near, a[at : at + 8, :], b[at : at + 8, :])

        k_own, k_in = block(near, far, 96), block(near, far, 104)
        k_halo = block(near_in, far_in, 96)
        k_face = jnp.minimum(k_own, k_halo)
        k_three = jnp.minimum(k_in, k_halo)
        own = [[block(near, far, (f * 3 + i) * 8) for i in range(3)] for f in range(4)]
        halo = [[block(near_in, far_in, (f * 3 + i) * 8) for i in range(3)] for f in range(4)]
        ws = []
        for i in range(3):
            c1, c2, c3 = terms[i]
            w = halo[2][i] * (c1 + c2 * halo[2][i]) + c3 * halo[3][i]
            ws.append(jnp.where(level_of[i] < k_halo, w, 0.0))
        group = 2.0 * (ws[0] + ws[1] + ws[2])
        total = group
        for shift in (8, 16, 32, 64):
            total = total + jnp.where(lane >= shift, roll(total, shift, 1), 0.0)
        above = jnp.where(lane >= 8, roll(total, 8, 1), 0.0)
        corr = [[None] * 3 for _ in range(4)]
        for i in range(3):
            press = above + ws[i]
            above = press + ws[i]
            flow = jnp.where(level_of[i] < k_face, r25, 0.0) * (own[0][i] + halo[0][i])
            inner = pin[24 * side + 8 * i : 24 * side + 8 * i + 8, :]
            slope = press - inner if side == 0 else inner - press
            slope = jnp.where(level_of[i] < k_three, 2.0 * r25, 0.0) * slope
            if side == 0:
                flow = -flow
            for f in range(4):
                corr[f][i] = flow * (own[f][i] + halo[f][i])
            corr[0][i] = corr[0][i] - slope
        sides.append(corr)
    packs = []
    for f in range(4):
        for i in range(3):
            packs += list(join_pairs(sides[0][f][i], sides[1][f][i], even))

    border = (lane == 0) | (lane == NI - 1)
    last_row, first_row = row == 7, row == 0
    bases, outs = (bu, bv, bt, bs), (ou, ov, ot, os)

    def step(q, carry):
        new = []
        for f in range(4):
            for i in range(3):
                k = q * 3 + i
                for half in range(2):
                    pack = carry[f * 6 + i * 2 + half]
                    for jh in range(4):
                        jt = 2 * jh + half
                        x = tile(bases[f], k, jt)
                        x = x + jnp.where(border, roll(pack, 127 - 2 * jh, 1), 0.0)
                        if jt == 0:
                            x = x + jnp.where(first_row, rows[1, f, pl.ds(k, 1), :], 0.0)
                        if jt == JT - 1:
                            x = x + jnp.where(last_row, rows[0, f, pl.ds(k, 1), :], 0.0)
                        buf[f, place(k, jt), :] = x
                    new.append(roll(pack, 120, 1))
        return tuple(new)

    carry = tuple(packs)
    copies = []
    for c in range(CH):
        carry = lax.fori_loop(c * NQ // CH, (c + 1) * NQ // CH, step, carry)
        for f in range(4):
            copy = pltpu.make_async_copy(
                buf.at[f, pl.ds(c * CK * NJ, CK * NJ)],
                outs[f].at[pl.ds(c * CK * NJ, CK * NJ)],
                sem.at[c, f],
            )
            copy.start()
            copies.append(copy)
    for copy in copies:
        copy.wait()


def near_core(x):
    return pltpu.with_memory_space_constraint(x, pltpu.VMEM)


def shards(u, v, t, s, kmt):
    nlon, nlat = lax.axis_size("lon"), lax.axis_size("lat")
    u, v, t, s = (x.reshape(NK * NJ, NI) for x in (u, v, t, s))
    field = jax.ShapeDtypeStruct((NK * NJ, NI), F32)
    params = pltpu.CompilerParams(vmem_limit_bytes=LIMIT)
    vfield = pltpu.VMEM((NK * NJ, NI), F32)
    column = pltpu.VMEM((112, NI), F32)
    strip = pltpu.VMEM((200, NI), F32)
    with jax.named_scope("pack"):
        *held, near, far, ra, rb = pl.pallas_call(
            pack_kernel,
            in_specs=[VM] + [ANY] * 4,
            out_specs=[VM] * 8,
            out_shape=[vfield] * 4 + [column] * 2 + [strip] * 2,
            scratch_shapes=[pltpu.SemaphoreType.DMA((CH, 4))],
            compiler_params=params,
            cost_estimate=pl.CostEstimate(
                flops=4_000_000, bytes_accessed=7_000_000, transcendentals=0
            ),
        )(kmt, u, v, t, s)

    held = [near_core(x) for x in held]

    def device(lon, lat):
        return lon * nlat + lat

    near_route = [(l, l ^ 1) for l in range(nlon)]
    far_route = [(l, (l + (1 if l % 2 else -1)) % nlon) for l in range(nlon)]
    a_route, b_route = [], []
    for l in range(nlon):
        for a in range(nlat):
            a_route.append((device(l, a), device(l, a ^ 1)))
            if a == 0:
                b_route.append((device(l, a), device(l ^ 1, a)))
            elif a == nlat - 1:
                b_route.append((device(l, a), device(nlon - 1 - l, a)))
            else:
                b_route.append((device(l, a), device(l, a + (1 if a % 2 else -1))))
    both = ("lon", "lat")
    with jax.named_scope("halo"):
        ra_in = lax.ppermute(ra, both, a_route)
        rb_in = lax.ppermute(rb, both, b_route)
        near_in = lax.ppermute(near, "lon", near_route)
        far_in = lax.ppermute(far, "lon", far_route)
    with jax.named_scope("inside"):
        *base, pin, p62, p1 = pl.pallas_call(
            main_kernel,
            in_specs=[VM] * 5,
            out_specs=[VM] * 7,
            out_shape=[vfield] * 4 + [pltpu.VMEM((NK, NI), F32)] * 3,
            scratch_shapes=[pltpu.VMEM((NJ, NI), F32)] * 7,
            compiler_params=params,
            cost_estimate=pl.CostEstimate(
                flops=40_000_000, bytes_accessed=13_000_000, transcendentals=0
            ),
        )(kmt, *held)
    base = [near_core(x) for x in base]
    rest = [near_core(x) for x in (pin, p62, p1, near, far, near_in, far_in, ra_in, rb_in)]
    with jax.named_scope("edges"):
        return tuple(
            x.reshape(NK, NJ, NI)
            for x in pl.pallas_call(
                fix_kernel,
                in_specs=[VM] * 18,
                out_specs=[ANY] * 4,
                out_shape=[field] * 4,
                scratch_shapes=[
                    pltpu.VMEM((4, NK * NJ, NI), F32),
                    pltpu.VMEM((2, 4, NK, NI), F32),
                    pltpu.SemaphoreType.DMA((CH, 4)),
                ],
                compiler_params=params,
                cost_estimate=pl.CostEstimate(
                    flops=4_000_000, bytes_accessed=7_000_000, transcendentals=0
                ),
            )(kmt, *held, *base, *rest)
        )


def solution(mesh):
    grid = P(None, "lat", "lon")
    return jax.shard_map(
        shards,
        mesh=mesh,
        in_specs=(grid,) * 4 + (P("lat", "lon"),),
        out_specs=(grid,) * 4,
        check_vma=False,
    )
```

```python
import math

import jax
import jax.numpy as jnp
from jax import lax
from jax.experimental import pallas as pl
from jax.experimental.pallas import tpu as pltpu
from jax.sharding import PartitionSpec as P

NK, NJ, NI = 48, 64, 128
JT = NJ // 8
NQ = NK // 3
CH = 4
CK = NK // CH
F32 = jnp.float32
VM = pl.BlockSpec(memory_space=pltpu.VMEM)
ANY = pl.BlockSpec(memory_space=pl.ANY)
LIMIT = 48 * 1024 * 1024


def lanes():
    return lax.broadcasted_iota(jnp.int32, (8, NI), 1)


def subs():
    return lax.broadcasted_iota(jnp.int32, (8, NI), 0)


def roll(x, shift, axis):
    return pltpu.roll(x, shift, axis)


def place(k, jt):
    return pl.ds(pl.multiple_of(k * NJ, NJ) + 8 * jt, 8)


def tile(ref, k, jt):
    return ref[place(k, jt), :]


def split_pairs(a, b, even):
    return jnp.where(even, a, roll(b, 1, 1)), jnp.where(even, roll(a, 127, 1), b)


def join_pairs(e, w, even):
    return jnp.where(even, e, roll(w, 1, 1)), jnp.where(even, roll(e, 127, 1), w)


def level_terms(k):
    h = 1.0 + k * (1.0 / NK)
    z = (k + 1.0) + k * (k + 1.0) * (0.5 / NK) - 0.5 * h
    return 0.5 * h * (-0.6 + 0.03 * z), -0.05 * h, 0.4 * h


def packed_latitude():
    row = lax.axis_index("lat") * NJ + (lanes() & 7) * 8 + subs()
    total = NJ * lax.axis_size("lat")
    phi = (-75.0 + 150.0 * (row.astype(F32) + 0.5) / total) * (math.pi / 180.0)
    return 1.0 / jnp.cos(phi), 1.5 * jnp.sin(phi)


def pack_kernel(kmt, u, v, t, s, uo, vo, to, so, near, far, ra, rb, sem):
    copies = [
        [
            pltpu.make_async_copy(
                src.at[pl.ds(c * CK * NJ, CK * NJ)],
                dst.at[pl.ds(c * CK * NJ, CK * NJ)],
                sem.at[c, f],
            )
            for f, (src, dst) in enumerate(((u, uo), (v, vo), (t, to), (s, so)))
        ]
        for c in range(CH)
    ]
    for group in copies:
        for copy in group:
            copy.start()
    lon, lat = lax.axis_index("lon"), lax.axis_index("lat")
    lon_even, lat_even = lon % 2 == 0, lat % 2 == 0
    lane = lanes()
    even = (lane & 1) == 0
    spot = [(lane >> 1) == 60 + jh for jh in range(4)]
    outs = (uo, vo, to, so)

    def put(acc, tiles):
        for jh in range(4):
            acc = jnp.where(spot[jh], roll(tiles[jh], 121 + 2 * jh, 1), acc)
        return acc

    kf = [kmt[8 * jt : 8 * jt + 8, :].astype(F32) for jt in range(JT)]
    inner = [
        jnp.minimum(x, jnp.where(lane == 0, roll(x, 127, 1), roll(x, 1, 1))) for x in kf
    ]
    zero = jnp.zeros((8, NI), F32)
    for at, tiles in ((96, kf), (104, inner)):
        e, w = split_pairs(put(zero, tiles[0::2]), put(zero, tiles[1::2]), even)
        for shift in (8, 16, 32, 64):
            e = e + roll(e, shift, 1)
            w = w + roll(w, shift, 1)
        near[at : at + 8, :] = jnp.where(lon_even, e, w)
        far[at : at + 8, :] = jnp.where(lon_even, w, e)

    def step(q, carry):
        new = []
        for f in range(4):
            for i in range(3):
                k = q * 3 + i
                for half in range(2):
                    acc = roll(carry[f * 6 + i * 2 + half], 120, 1)
                    tiles = [tile(outs[f], k, jt) for jt in range(half, JT, 2)]
                    new.append(put(acc, tiles))
        return tuple(new)

    carry = (zero,) * 24
    for c in range(CH):
        for copy in copies[c]:
            copy.wait()
        carry = lax.fori_loop(c * NQ // CH, (c + 1) * NQ // CH, step, carry)
    for f in range(4):
        for i in range(3):
            e, w = split_pairs(carry[f * 6 + i * 2], carry[f * 6 + i * 2 + 1], even)
            at = (f * 3 + i) * 8
            near[at : at + 8, :] = jnp.where(lon_even, e, w)
            far[at : at + 8, :] = jnp.where(lon_even, w, e)

    fold = lat == lax.axis_size("lat") - 1
    order = jnp.where(fold, 127 - lane, lane)
    tops, bottoms = [], []
    for ref in outs:
        top = ref[pl.ds(NJ - 1, NK, stride=NJ), :]
        bottom = ref[pl.ds(0, NK, stride=NJ), :]
        for b in range(6):
            tops.append(top[8 * b : 8 * b + 8, :])
            bottoms.append(bottom[8 * b : 8 * b + 8, :])
    tops.append(jnp.broadcast_to(kf[JT - 1][7:8, :], (8, NI)))
    bottoms.append(jnp.broadcast_to(kf[0][0:1, :], (8, NI)))
    for n, (top, bottom) in enumerate(zip(tops, bottoms)):
        ra[8 * n : 8 * n + 8, :] = jnp.where(lat_even, top, bottom)
        rb[8 * n : 8 * n + 8, :] = jnp.take_along_axis(
            jnp.where(lat_even, bottom, top), order, axis=1, mode="promise_in_bounds"
        )


def main_kernel(
    kmt, u_ref, v_ref, t_ref, s_ref, ou, ov, ot, os, pin, p62, p1, ks, ke, kn, kew, kns, rs, fs, pins
):
    kf = kmt[...].astype(F32)
    lane64 = lax.broadcasted_iota(jnp.int32, (NJ, NI), 1)
    row64 = lax.broadcasted_iota(jnp.int32, (NJ, NI), 0)
    k_e = jnp.minimum(kf, roll(kf, 127, 1))
    k_w = roll(kf, 1, 1)
    k_n = jnp.minimum(kf, roll(kf, NJ - 1, 0))
    k_s = roll(kf, 1, 0)
    ks[...] = kf
    ke[...] = jnp.where(lane64 == NI - 1, 0.0, k_e)
    kew[...] = jnp.where((lane64 == 0) | (lane64 == NI - 1), 0.0, jnp.minimum(k_e, k_w))
    kn[...] = jnp.where(row64 == NJ - 1, 0.0, k_n)
    kns[...] = jnp.where((row64 == 0) | (row64 == NJ - 1), 0.0, jnp.minimum(k_n, k_s))
    r, f = packed_latitude()
    for jt in range(JT):
        rs[8 * jt : 8 * jt + 8, :] = jnp.broadcast_to(0.025 * r[:, jt : jt + 1], (8, NI))
        fs[8 * jt : 8 * jt + 8, :] = jnp.broadcast_to(0.1 * f[:, jt : jt + 1], (8, NI))

    lane, row = lanes(), subs()
    first, row0, row7 = lane == 0, row == 0, row == 7
    even = (lane & 1) == 0
    spot = [(lane >> 1) == 60 + jh for jh in range(4)]
    zero = jnp.zeros((8, NI), F32)

    def fixed(ref, jt):
        return ref[8 * jt : 8 * jt + 8, :]

    def north(now, after):
        return roll(jnp.where(row0, after, now), 7, 0)

    def south(now, before):
        return roll(jnp.where(row7, before, now), 1, 0)

    def level(k, acc):
        kk = k.astype(F32)
        c1, c2, c3 = level_terms(kk)
        press, acc_new = [], []
        for jt in range(JT):
            t = tile(t_ref, k, jt)
            w = t * (c1 + c2 * t) + c3 * tile(s_ref, k, jt)
            w = jnp.where(fixed(ks, jt) > kk, w, 0.0)
            p = acc[jt] + w
            press.append(p)
            acc_new.append(p + w)
        p62[pl.ds(k, 1), :] = press[JT - 1][6:7, :]
        p1[pl.ds(k, 1), :] = press[0][1:2, :]
        edge = [zero, zero]
        before = [zero] * 4
        for jt in range(JT):
            q = [tile(ref, k, jt) for ref in (u_ref, v_ref, t_ref, s_ref)]
            up = min(jt + 1, JT - 1)
            r25, f01 = fixed(rs, jt), fixed(fs, jt)
            qe = [x + roll(x, 127, 1) for x in q]
            flow = jnp.where(fixed(ke, jt) > kk, r25, 0.0) * qe[0]
            fe = [flow * x for x in qe]
            qn = [
                x + north(x, tile(ref, k, up)) for x, ref in zip(q, (u_ref, v_ref, t_ref, s_ref))
            ]
            flow = jnp.where(fixed(kn, jt) > kk, 0.025, 0.0) * qn[1]
            fn = [flow * x for x in qn]
            out = [
                x - (a - roll(a, 1, 1)) - (b - south(b, c))
                for x, a, b, c in zip(q, fe, fn, before)
            ]
            before = fn
            p = press[jt]
            pe, pw = roll(p, 127, 1), roll(p, 1, 1)
            spot_p = roll(jnp.where(first, pe, pw), 121 + 2 * (jt // 2), 1)
            edge[jt % 2] = jnp.where(spot[jt // 2], spot_p, edge[jt % 2])
            slope = jnp.where(fixed(kew, jt) > kk, 2.0 * r25, 0.0) * (pe - pw)
            out[0] = out[0] + (f01 * q[1] - slope)
            pn, ps = north(p, press[up]), south(p, press[max(jt - 1, 0)])
            slope = jnp.where(fixed(kns, jt) > kk, 0.05, 0.0) * (pn - ps)
            out[1] = out[1] - (f01 * q[0] + slope)
            wet = fixed(ks, jt) > kk
            for ref, x in zip((ou, ov, ot, os), out):
                ref[place(k, jt), :] = jnp.where(wet, x, 0.0)
        for half in range(2):
            pins[pl.ds(pl.multiple_of(k * 16, 16) + 8 * half, 8), :] = edge[half]
        return tuple(acc_new)

    lax.fori_loop(0, NK, level, (zero,) * JT)

    def gather(q, carry):
        at = pl.multiple_of(q * 48, 48)
        return tuple(
            roll(x, 120, 1) + pins[pl.ds(at + 8 * n, 8), :] for n, x in enumerate(carry)
        )

    pairs = lax.fori_loop(0, NQ, gather, (zero,) * 6)
    for i in range(3):
        e, w = split_pairs(pairs[2 * i], pairs[2 * i + 1], even)
        pin[8 * i : 8 * i + 8, :] = e
        pin[24 + 8 * i : 32 + 8 * i, :] = w


def fix_kernel(
    kmt, u_ref, v_ref, t_ref, s_ref, bu, bv, bt, bs, pin, p62, p1,
    near, far, near_in, far_in, ra_in, rb_in, ou, ov, ot, os, buf, rows, sem,
):
    lon, lat = lax.axis_index("lon"), lax.axis_index("lat")
    lon_even, lat_even = lon % 2 == 0, lat % 2 == 0
    is_top, is_bottom = lat == lax.axis_size("lat") - 1, lat == 0
    lane, row = lanes(), subs()
    even = (lane & 1) == 0
    fields = (u_ref, v_ref, t_ref, s_ref)

    level48 = lax.broadcasted_iota(jnp.int32, (NK, NI), 0).astype(F32)
    row48 = lax.broadcasted_iota(jnp.int32, (NK, NI), 0)
    c1, c2, c3 = level_terms(level48)
    sign = jnp.where(is_top, -1.0, 1.0)
    for side in range(2):
        own_row, next_row = (NJ - 1, NJ - 2) if side == 0 else (0, 1)
        use_a = lat_even if side == 0 else jnp.logical_not(lat_even)
        halo = [
            jnp.where(use_a, ra_in[NK * f : NK * f + NK, :], rb_in[NK * f : NK * f + NK, :])
            for f in range(4)
        ]
        k_halo = jnp.where(use_a, ra_in[4 * NK : 4 * NK + 1, :], rb_in[4 * NK : 4 * NK + 1, :])
        if side == 0:
            halo[0], halo[1] = halo[0] * sign, halo[1] * sign
        else:
            k_halo = jnp.where(is_bottom, 0.0, k_halo)
        own = [
            ref[pl.ds(own_row, NK, stride=NJ), :] for ref in fields
        ]
        k_own = kmt[own_row : own_row + 1, :].astype(F32)
        k_next = kmt[next_row : next_row + 1, :].astype(F32)
        k_face = jnp.minimum(k_own, k_halo)
        w = halo[2] * (c1 + c2 * halo[2]) + c3 * halo[3]
        w = jnp.where(level48 < k_halo, w, 0.0)
        total = w + w
        shift = 1
        while shift < NK:
            total = total + jnp.where(row48 >= shift, roll(total, shift, 0), 0.0)
            shift *= 2
        press = total - w
        flow = jnp.where(level48 < k_face, 0.025, 0.0) * (own[1] + halo[1])
        if side == 0:
            flow = -flow
        slope = press - p62[...] if side == 0 else p1[...] - press
        slope = jnp.where(level48 < jnp.minimum(k_face, k_next), 0.05, 0.0) * slope
        for f in range(4):
            add = flow * (own[f] + halo[f])
            if f == 1:
                add = add - slope
            rows[side, f, :, :] = add

    r, _ = packed_latitude()
    r25 = 0.025 * r
    level_of = [((lane >> 3) * 3 + i).astype(F32) for i in range(3)]
    terms = [level_terms(x) for x in level_of]
    sides = []
    for side in range(2):
        use_near = lon_even if side == 0 else jnp.logical_not(lon_even)

        def block(a, b, at):
            return jnp.where(use_near, a[at : at + 8, :], b[at : at + 8, :])

        k_own, k_in = block(near, far, 96), block(near, far, 104)
        k_halo = block(near_in, far_in, 96)
        k_face = jnp.minimum(k_own, k_halo)
        k_three = jnp.minimum(k_in, k_halo)
        own = [[block(near, far, (f * 3 + i) * 8) for i in range(3)] for f in range(4)]
        halo = [[block(near_in, far_in, (f * 3 + i) * 8) for i in range(3)] for f in range(4)]
        ws = []
        for i in range(3):
            c1, c2, c3 = terms[i]
            w = halo[2][i] * (c1 + c2 * halo[2][i]) + c3 * halo[3][i]
            ws.append(jnp.where(level_of[i] < k_halo, w, 0.0))
        group = 2.0 * (ws[0] + ws[1] + ws[2])
        total = group
        for shift in (8, 16, 32, 64):
            total = total + jnp.where(lane >= shift, roll(total, shift, 1), 0.0)
        above = jnp.where(lane >= 8, roll(total, 8, 1), 0.0)
        corr = [[None] * 3 for _ in range(4)]
        for i in range(3):
            press = above + ws[i]
            above = press + ws[i]
            flow = jnp.where(level_of[i] < k_face, r25, 0.0) * (own[0][i] + halo[0][i])
            inner = pin[24 * side + 8 * i : 24 * side + 8 * i + 8, :]
            slope = press - inner if side == 0 else inner - press
            slope = jnp.where(level_of[i] < k_three, 2.0 * r25, 0.0) * slope
            if side == 0:
                flow = -flow
            for f in range(4):
                corr[f][i] = flow * (own[f][i] + halo[f][i])
            corr[0][i] = corr[0][i] - slope
        sides.append(corr)
    packs = []
    for f in range(4):
        for i in range(3):
            packs += list(join_pairs(sides[0][f][i], sides[1][f][i], even))

    border = (lane == 0) | (lane == NI - 1)
    last_row, first_row = row == 7, row == 0
    bases, outs = (bu, bv, bt, bs), (ou, ov, ot, os)

    def step(q, carry):
        new = []
        for f in range(4):
            for i in range(3):
                k = q * 3 + i
                for half in range(2):
                    pack = carry[f * 6 + i * 2 + half]
                    for jh in range(4):
                        jt = 2 * jh + half
                        x = tile(bases[f], k, jt)
                        x = x + jnp.where(border, roll(pack, 127 - 2 * jh, 1), 0.0)
                        if jt == 0:
                            x = x + jnp.where(first_row, rows[1, f, pl.ds(k, 1), :], 0.0)
                        if jt == JT - 1:
                            x = x + jnp.where(last_row, rows[0, f, pl.ds(k, 1), :], 0.0)
                        buf[f, place(k, jt), :] = x
                    new.append(roll(pack, 120, 1))
        return tuple(new)

    carry = tuple(packs)
    copies = []
    for c in range(CH):
        carry = lax.fori_loop(c * NQ // CH, (c + 1) * NQ // CH, step, carry)
        for f in range(4):
            copy = pltpu.make_async_copy(
                buf.at[f, pl.ds(c * CK * NJ, CK * NJ)],
                outs[f].at[pl.ds(c * CK * NJ, CK * NJ)],
                sem.at[c, f],
            )
            copy.start()
            copies.append(copy)
    for copy in copies:
        copy.wait()


def near_core(x):
    return pltpu.with_memory_space_constraint(x, pltpu.VMEM)


def shards(u, v, t, s, kmt):
    nlon, nlat = lax.axis_size("lon"), lax.axis_size("lat")
    u, v, t, s = (x.reshape(NK * NJ, NI) for x in (u, v, t, s))
    field = jax.ShapeDtypeStruct((NK * NJ, NI), F32)
    params = pltpu.CompilerParams(vmem_limit_bytes=LIMIT)
    vfield = pltpu.VMEM((NK * NJ, NI), F32)
    column = pltpu.VMEM((112, NI), F32)
    strip = pltpu.VMEM((200, NI), F32)
    with jax.named_scope("pack"):
        *held, near, far, ra, rb = pl.pallas_call(
            pack_kernel,
            in_specs=[VM] + [ANY] * 4,
            out_specs=[VM] * 8,
            out_shape=[vfield] * 4 + [column] * 2 + [strip] * 2,
            scratch_shapes=[pltpu.SemaphoreType.DMA((CH, 4))],
            compiler_params=params,
            cost_estimate=pl.CostEstimate(
                flops=4_000_000, bytes_accessed=7_000_000, transcendentals=0
            ),
        )(kmt, u, v, t, s)

    held = [near_core(x) for x in held]

    def device(lon, lat):
        return lon * nlat + lat

    near_route = [(l, l ^ 1) for l in range(nlon)]
    far_route = [(l, (l + (1 if l % 2 else -1)) % nlon) for l in range(nlon)]
    a_route, b_route = [], []
    for l in range(nlon):
        for a in range(nlat):
            a_route.append((device(l, a), device(l, a ^ 1)))
            if a == 0:
                b_route.append((device(l, a), device(l ^ 1, a)))
            elif a == nlat - 1:
                b_route.append((device(l, a), device(nlon - 1 - l, a)))
            else:
                b_route.append((device(l, a), device(l, a + (1 if a % 2 else -1))))
    both = ("lon", "lat")
    with jax.named_scope("halo"):
        ra_in = lax.ppermute(ra, both, a_route)
        rb_in = lax.ppermute(rb, both, b_route)
        near_in = lax.ppermute(near, "lon", near_route)
        far_in = lax.ppermute(far, "lon", far_route)
    with jax.named_scope("inside"):
        *base, pin, p62, p1 = pl.pallas_call(
            main_kernel,
            in_specs=[VM] * 5,
            out_specs=[VM] * 7,
            out_shape=[vfield] * 4 + [pltpu.VMEM((NK, NI), F32)] * 3,
            scratch_shapes=[pltpu.VMEM((NJ, NI), F32)] * 7 + [pltpu.VMEM((NK * 16, NI), F32)],
            compiler_params=params,
            cost_estimate=pl.CostEstimate(
                flops=40_000_000, bytes_accessed=13_000_000, transcendentals=0
            ),
        )(kmt, *held)
    base = [near_core(x) for x in base]
    rest = [near_core(x) for x in (pin, p62, p1, near, far, near_in, far_in, ra_in, rb_in)]
    with jax.named_scope("edges"):
        return tuple(
            x.reshape(NK, NJ, NI)
            for x in pl.pallas_call(
                fix_kernel,
                in_specs=[VM] * 18,
                out_specs=[ANY] * 4,
                out_shape=[field] * 4,
                scratch_shapes=[
                    pltpu.VMEM((4, NK * NJ, NI), F32),
                    pltpu.VMEM((2, 4, NK, NI), F32),
                    pltpu.SemaphoreType.DMA((CH, 4)),
                ],
                compiler_params=params,
                cost_estimate=pl.CostEstimate(
                    flops=4_000_000, bytes_accessed=7_000_000, transcendentals=0
                ),
            )(kmt, *held, *base, *rest)
        )


def solution(mesh):
    grid = P(None, "lat", "lon")
    return jax.shard_map(
        shards,
        mesh=mesh,
        in_specs=(grid,) * 4 + (P("lat", "lon"),),
        out_specs=(grid,) * 4,
        check_vma=False,
    )
```

```python
import math

import jax
import jax.numpy as jnp
from jax import lax
from jax.experimental import pallas as pl
from jax.experimental.pallas import tpu as pltpu
from jax.sharding import PartitionSpec as P

NK, NJ, NI = 48, 64, 128
JT = NJ // 8
NQ = NK // 3
CH = 4
CK = NK // CH
F32 = jnp.float32
VM = pl.BlockSpec(memory_space=pltpu.VMEM)
ANY = pl.BlockSpec(memory_space=pl.ANY)
LIMIT = 48 * 1024 * 1024


def lanes():
    return lax.broadcasted_iota(jnp.int32, (8, NI), 1)


def subs():
    return lax.broadcasted_iota(jnp.int32, (8, NI), 0)


def roll(x, shift, axis):
    return pltpu.roll(x, shift, axis)


def place(k, jt):
    return pl.ds(pl.multiple_of(k * NJ, NJ) + 8 * jt, 8)


def tile(ref, k, jt):
    return ref[place(k, jt), :]


def split_pairs(a, b, even):
    return jnp.where(even, a, roll(b, 1, 1)), jnp.where(even, roll(a, 127, 1), b)


def join_pairs(e, w, even):
    return jnp.where(even, e, roll(w, 1, 1)), jnp.where(even, roll(e, 127, 1), w)


def level_terms(k):
    h = 1.0 + k * (1.0 / NK)
    z = (k + 1.0) + k * (k + 1.0) * (0.5 / NK) - 0.5 * h
    return 0.5 * h * (-0.6 + 0.03 * z), -0.05 * h, 0.4 * h


def packed_latitude():
    row = lax.axis_index("lat") * NJ + (lanes() & 7) * 8 + subs()
    total = NJ * lax.axis_size("lat")
    phi = (-75.0 + 150.0 * (row.astype(F32) + 0.5) / total) * (math.pi / 180.0)
    return 1.0 / jnp.cos(phi), 1.5 * jnp.sin(phi)


def pack_kernel(kmt, u, v, t, s, uo, vo, to, so, near, far, ra, rb, sem):
    copies = [
        [
            pltpu.make_async_copy(
                src.at[pl.ds(c * CK * NJ, CK * NJ)],
                dst.at[pl.ds(c * CK * NJ, CK * NJ)],
                sem.at[c, f],
            )
            for f, (src, dst) in enumerate(((u, uo), (v, vo), (t, to), (s, so)))
        ]
        for c in range(CH)
    ]
    for group in copies:
        for copy in group:
            copy.start()
    lon, lat = lax.axis_index("lon"), lax.axis_index("lat")
    lon_even, lat_even = lon % 2 == 0, lat % 2 == 0
    lane = lanes()
    even = (lane & 1) == 0
    spot = [(lane >> 1) == 60 + jh for jh in range(4)]
    outs = (uo, vo, to, so)

    def put(acc, tiles):
        for jh in range(4):
            acc = jnp.where(spot[jh], roll(tiles[jh], 121 + 2 * jh, 1), acc)
        return acc

    kf = [kmt[8 * jt : 8 * jt + 8, :].astype(F32) for jt in range(JT)]
    inner = [
        jnp.minimum(x, jnp.where(lane == 0, roll(x, 127, 1), roll(x, 1, 1))) for x in kf
    ]
    zero = jnp.zeros((8, NI), F32)
    for at, tiles in ((96, kf), (104, inner)):
        e, w = split_pairs(put(zero, tiles[0::2]), put(zero, tiles[1::2]), even)
        for shift in (8, 16, 32, 64):
            e = e + roll(e, shift, 1)
            w = w + roll(w, shift, 1)
        near[at : at + 8, :] = jnp.where(lon_even, e, w)
        far[at : at + 8, :] = jnp.where(lon_even, w, e)

    def step(q, carry):
        new = []
        for f in range(4):
            for i in range(3):
                k = q * 3 + i
                for half in range(2):
                    acc = roll(carry[f * 6 + i * 2 + half], 120, 1)
                    tiles = [tile(outs[f], k, jt) for jt in range(half, JT, 2)]
                    new.append(put(acc, tiles))
        return tuple(new)

    carry = (zero,) * 24
    for c in range(CH):
        for copy in copies[c]:
            copy.wait()
        carry = lax.fori_loop(c * NQ // CH, (c + 1) * NQ // CH, step, carry, unroll=4)
    for f in range(4):
        for i in range(3):
            e, w = split_pairs(carry[f * 6 + i * 2], carry[f * 6 + i * 2 + 1], even)
            at = (f * 3 + i) * 8
            near[at : at + 8, :] = jnp.where(lon_even, e, w)
            far[at : at + 8, :] = jnp.where(lon_even, w, e)

    fold = lat == lax.axis_size("lat") - 1
    order = jnp.where(fold, 127 - lane, lane)
    tops, bottoms = [], []
    for ref in outs:
        top = ref[pl.ds(NJ - 1, NK, stride=NJ), :]
        bottom = ref[pl.ds(0, NK, stride=NJ), :]
        for b in range(6):
            tops.append(top[8 * b : 8 * b + 8, :])
            bottoms.append(bottom[8 * b : 8 * b + 8, :])
    tops.append(jnp.broadcast_to(kf[JT - 1][7:8, :], (8, NI)))
    bottoms.append(jnp.broadcast_to(kf[0][0:1, :], (8, NI)))
    for n, (top, bottom) in enumerate(zip(tops, bottoms)):
        ra[8 * n : 8 * n + 8, :] = jnp.where(lat_even, top, bottom)
        rb[8 * n : 8 * n + 8, :] = jnp.take_along_axis(
            jnp.where(lat_even, bottom, top), order, axis=1, mode="promise_in_bounds"
        )


def main_kernel(
    kmt, u_ref, v_ref, t_ref, s_ref, ou, ov, ot, os, pin, p62, p1, ks, ke, kn, kew, kns, rs, fs, pins, press, flux, rise, inner
):
    kf = kmt[...].astype(F32)
    lane64 = lax.broadcasted_iota(jnp.int32, (NJ, NI), 1)
    row64 = lax.broadcasted_iota(jnp.int32, (NJ, NI), 0)
    k_e = jnp.minimum(kf, roll(kf, 127, 1))
    k_w = roll(kf, 1, 1)
    k_n = jnp.minimum(kf, roll(kf, NJ - 1, 0))
    k_s = roll(kf, 1, 0)
    ks[...] = kf
    ke[...] = jnp.where(lane64 == NI - 1, 0.0, k_e)
    kew[...] = jnp.where((lane64 == 0) | (lane64 == NI - 1), 0.0, jnp.minimum(k_e, k_w))
    kn[...] = jnp.where(row64 == NJ - 1, 0.0, k_n)
    kns[...] = jnp.where((row64 == 0) | (row64 == NJ - 1), 0.0, jnp.minimum(k_n, k_s))
    r, f = packed_latitude()
    for jt in range(JT):
        rs[8 * jt : 8 * jt + 8, :] = jnp.broadcast_to(0.025 * r[:, jt : jt + 1], (8, NI))
        fs[8 * jt : 8 * jt + 8, :] = jnp.broadcast_to(0.1 * f[:, jt : jt + 1], (8, NI))

    lane, row = lanes(), subs()
    first = lane == 0
    even = (lane & 1) == 0
    spot = [(lane >> 1) == 60 + jh for jh in range(4)]
    zero = jnp.zeros((8, NI), F32)

    def fixed(ref, jt):
        return ref[8 * jt : 8 * jt + 8, :]

    def after(ref, x, k, jt):
        if jt == JT - 1:
            return roll(x, 7, 0)
        return ref[pl.ds(pl.multiple_of(k * NJ, NJ) + 8 * jt + 1, 8), :]

    fields, outs = (u_ref, v_ref, t_ref, s_ref), (ou, ov, ot, os)

    def open_level(k, acc):
        kk = k.astype(F32)
        c1, c2, c3 = level_terms(kk)
        acc_new = []
        for jt in range(JT):
            q = [tile(ref, k, jt) for ref in fields]
            w = q[2] * (c1 + c2 * q[2]) + c3 * q[3]
            w = jnp.where(fixed(ks, jt) > kk, w, 0.0)
            p = acc[jt] + w
            press[8 + 8 * jt : 16 + 8 * jt, :] = p
            acc_new.append(p + w)
            qe = [x + roll(x, 127, 1) for x in q]
            flow = jnp.where(fixed(ke, jt) > kk, fixed(rs, jt), 0.0) * qe[0]
            for f in range(4):
                flux[f, 8 * jt : 8 * jt + 8, :] = flow * qe[f]
            qn = [x + after(ref, x, k, jt) for x, ref in zip(q, fields)]
            flow = jnp.where(fixed(kn, jt) > kk, 0.025, 0.0) * qn[1]
            for f in range(4):
                rise[f, 8 + 8 * jt : 16 + 8 * jt, :] = flow * qn[f]
        return tuple(acc_new)

    def close_level(k):
        kk = k.astype(F32)
        p62[pl.ds(k, 1), :] = press[8 + NJ - 2 : 8 + NJ - 1, :]
        p1[pl.ds(k, 1), :] = press[9:10, :]
        for jt in range(JT):
            q = [tile(ref, k, jt) for ref in fields]
            f01 = fixed(fs, jt)
            fe = [flux[f, 8 * jt : 8 * jt + 8, :] for f in range(4)]
            fn = [rise[f, 8 + 8 * jt : 16 + 8 * jt, :] for f in range(4)]
            fs_ = [rise[f, 7 + 8 * jt : 15 + 8 * jt, :] for f in range(4)]
            out = [
                x - (a - roll(a, 1, 1)) - (b - c) for x, a, b, c in zip(q, fe, fn, fs_)
            ]
            p = press[8 + 8 * jt : 16 + 8 * jt, :]
            pe, pw = roll(p, 127, 1), roll(p, 1, 1)
            inner[8 * jt : 8 * jt + 8, :] = jnp.where(first, pe, pw)
            slope = jnp.where(fixed(kew, jt) > kk, 2.0 * fixed(rs, jt), 0.0) * (pe - pw)
            out[0] = out[0] + (f01 * q[1] - slope)
            pn = press[9 + 8 * jt : 17 + 8 * jt, :]
            ps = press[7 + 8 * jt : 15 + 8 * jt, :]
            slope = jnp.where(fixed(kns, jt) > kk, 0.05, 0.0) * (pn - ps)
            out[1] = out[1] - (f01 * q[0] + slope)
            wet = fixed(ks, jt) > kk
            for ref, x in zip(outs, out):
                ref[place(k, jt), :] = jnp.where(wet, x, 0.0)

    def pack_inner(k):
        for half in range(2):
            edge = zero
            for jh in range(4):
                x = roll(fixed(inner, 2 * jh + half), 121 + 2 * jh, 1)
                edge = jnp.where(spot[jh], x, edge)
            pins[pl.ds(pl.multiple_of(k * 16, 16) + 8 * half, 8), :] = edge

    def level(k, acc):
        pack_inner(k)
        close_level(k)
        return open_level(jnp.minimum(k + 1, NK - 1), acc)

    inner[...] = jnp.zeros((NJ, NI), F32)
    press[0:8, :] = zero
    press[8 + NJ : 16 + NJ, :] = zero
    for f in range(4):
        rise[f, 0:8, :] = zero
    lax.fori_loop(0, NK, level, open_level(jnp.int32(0), (zero,) * JT))
    pack_inner(jnp.int32(NK))

    def gather(q, carry):
        at = pl.multiple_of(q * 48, 16) + 16
        return tuple(
            roll(x, 120, 1) + pins[pl.ds(at + 8 * n, 8), :] for n, x in enumerate(carry)
        )

    pairs = lax.fori_loop(0, NQ, gather, (zero,) * 6)
    for i in range(3):
        e, w = split_pairs(pairs[2 * i], pairs[2 * i + 1], even)
        pin[8 * i : 8 * i + 8, :] = e
        pin[24 + 8 * i : 32 + 8 * i, :] = w


def fix_kernel(
    kmt, u_ref, v_ref, t_ref, s_ref, bu, bv, bt, bs, pin, p62, p1,
    near, far, near_in, far_in, ra_in, rb_in, ou, ov, ot, os, buf, rows, sem,
):
    lon, lat = lax.axis_index("lon"), lax.axis_index("lat")
    lon_even, lat_even = lon % 2 == 0, lat % 2 == 0
    is_top, is_bottom = lat == lax.axis_size("lat") - 1, lat == 0
    lane, row = lanes(), subs()
    even = (lane & 1) == 0
    fields = (u_ref, v_ref, t_ref, s_ref)

    level48 = lax.broadcasted_iota(jnp.int32, (NK, NI), 0).astype(F32)
    row48 = lax.broadcasted_iota(jnp.int32, (NK, NI), 0)
    c1, c2, c3 = level_terms(level48)
    sign = jnp.where(is_top, -1.0, 1.0)
    for side in range(2):
        own_row, next_row = (NJ - 1, NJ - 2) if side == 0 else (0, 1)
        use_a = lat_even if side == 0 else jnp.logical_not(lat_even)
        halo = [
            jnp.where(use_a, ra_in[NK * f : NK * f + NK, :], rb_in[NK * f : NK * f + NK, :])
            for f in range(4)
        ]
        k_halo = jnp.where(use_a, ra_in[4 * NK : 4 * NK + 1, :], rb_in[4 * NK : 4 * NK + 1, :])
        if side == 0:
            halo[0], halo[1] = halo[0] * sign, halo[1] * sign
        else:
            k_halo = jnp.where(is_bottom, 0.0, k_halo)
        own = [
            ref[pl.ds(own_row, NK, stride=NJ), :] for ref in fields
        ]
        k_own = kmt[own_row : own_row + 1, :].astype(F32)
        k_next = kmt[next_row : next_row + 1, :].astype(F32)
        k_face = jnp.minimum(k_own, k_halo)
        w = halo[2] * (c1 + c2 * halo[2]) + c3 * halo[3]
        w = jnp.where(level48 < k_halo, w, 0.0)
        total = w + w
        shift = 1
        while shift < NK:
            total = total + jnp.where(row48 >= shift, roll(total, shift, 0), 0.0)
            shift *= 2
        press = total - w
        flow = jnp.where(level48 < k_face, 0.025, 0.0) * (own[1] + halo[1])
        if side == 0:
            flow = -flow
        slope = press - p62[...] if side == 0 else p1[...] - press
        slope = jnp.where(level48 < jnp.minimum(k_face, k_next), 0.05, 0.0) * slope
        for f in range(4):
            add = flow * (own[f] + halo[f])
            if f == 1:
                add = add - slope
            rows[side, f, :, :] = add

    r, _ = packed_latitude()
    r25 = 0.025 * r
    level_of = [((lane >> 3) * 3 + i).astype(F32) for i in range(3)]
    terms = [level_terms(x) for x in level_of]
    sides = []
    for side in range(2):
        use_near = lon_even if side == 0 else jnp.logical_not(lon_even)

        def block(a, b, at):
            return jnp.where(use_near, a[at : at + 8, :], b[at : at + 8, :])

        k_own, k_in = block(near, far, 96), block(near, far, 104)
        k_halo = block(near_in, far_in, 96)
        k_face = jnp.minimum(k_own, k_halo)
        k_three = jnp.minimum(k_in, k_halo)
        own = [[block(near, far, (f * 3 + i) * 8) for i in range(3)] for f in range(4)]
        halo = [[block(near_in, far_in, (f * 3 + i) * 8) for i in range(3)] for f in range(4)]
        ws = []
        for i in range(3):
            c1, c2, c3 = terms[i]
            w = halo[2][i] * (c1 + c2 * halo[2][i]) + c3 * halo[3][i]
            ws.append(jnp.where(level_of[i] < k_halo, w, 0.0))
        group = 2.0 * (ws[0] + ws[1] + ws[2])
        total = group
        for shift in (8, 16, 32, 64):
            total = total + jnp.where(lane >= shift, roll(total, shift, 1), 0.0)
        above = jnp.where(lane >= 8, roll(total, 8, 1), 0.0)
        corr = [[None] * 3 for _ in range(4)]
        for i in range(3):
            press = above + ws[i]
            above = press + ws[i]
            flow = jnp.where(level_of[i] < k_face, r25, 0.0) * (own[0][i] + halo[0][i])
            inner = pin[24 * side + 8 * i : 24 * side + 8 * i + 8, :]
            slope = press - inner if side == 0 else inner - press
            slope = jnp.where(level_of[i] < k_three, 2.0 * r25, 0.0) * slope
            if side == 0:
                flow = -flow
            for f in range(4):
                corr[f][i] = flow * (own[f][i] + halo[f][i])
            corr[0][i] = corr[0][i] - slope
        sides.append(corr)
    packs = []
    for f in range(4):
        for i in range(3):
            packs += list(join_pairs(sides[0][f][i], sides[1][f][i], even))

    border = (lane == 0) | (lane == NI - 1)
    last_row, first_row = row == 7, row == 0
    bases, outs = (bu, bv, bt, bs), (ou, ov, ot, os)

    def step(q, carry):
        new = []
        for f in range(4):
            for i in range(3):
                k = q * 3 + i
                for half in range(2):
                    pack = carry[f * 6 + i * 2 + half]
                    for jh in range(4):
                        jt = 2 * jh + half
                        x = tile(bases[f], k, jt)
                        x = x + jnp.where(border, roll(pack, 127 - 2 * jh, 1), 0.0)
                        if jt == 0:
                            x = x + jnp.where(first_row, rows[1, f, pl.ds(k, 1), :], 0.0)
                        if jt == JT - 1:
                            x = x + jnp.where(last_row, rows[0, f, pl.ds(k, 1), :], 0.0)
                        buf[f, place(k, jt), :] = x
                    new.append(roll(pack, 120, 1))
        return tuple(new)

    carry = tuple(packs)
    copies = []
    for c in range(CH):
        carry = lax.fori_loop(c * NQ // CH, (c + 1) * NQ // CH, step, carry, unroll=4)
        for f in range(4):
            copy = pltpu.make_async_copy(
                buf.at[f, pl.ds(c * CK * NJ, CK * NJ)],
                outs[f].at[pl.ds(c * CK * NJ, CK * NJ)],
                sem.at[c, f],
            )
            copy.start()
            copies.append(copy)
    for copy in copies:
        copy.wait()


def near_core(x):
    return pltpu.with_memory_space_constraint(x, pltpu.VMEM)


def shards(u, v, t, s, kmt):
    nlon, nlat = lax.axis_size("lon"), lax.axis_size("lat")
    u, v, t, s = (x.reshape(NK * NJ, NI) for x in (u, v, t, s))
    field = jax.ShapeDtypeStruct((NK * NJ, NI), F32)
    params = pltpu.CompilerParams(vmem_limit_bytes=LIMIT)
    vfield = pltpu.VMEM((NK * NJ, NI), F32)
    column = pltpu.VMEM((112, NI), F32)
    strip = pltpu.VMEM((200, NI), F32)
    with jax.named_scope("pack"):
        *held, near, far, ra, rb = pl.pallas_call(
            pack_kernel,
            in_specs=[VM] + [ANY] * 4,
            out_specs=[VM] * 8,
            out_shape=[vfield] * 4 + [column] * 2 + [strip] * 2,
            scratch_shapes=[pltpu.SemaphoreType.DMA((CH, 4))],
            compiler_params=params,
            cost_estimate=pl.CostEstimate(
                flops=4_000_000, bytes_accessed=7_000_000, transcendentals=0
            ),
        )(kmt, u, v, t, s)

    held = [near_core(x) for x in held]

    def device(lon, lat):
        return lon * nlat + lat

    near_route = [(l, l ^ 1) for l in range(nlon)]
    far_route = [(l, (l + (1 if l % 2 else -1)) % nlon) for l in range(nlon)]
    a_route, b_route = [], []
    for l in range(nlon):
        for a in range(nlat):
            a_route.append((device(l, a), device(l, a ^ 1)))
            if a == 0:
                b_route.append((device(l, a), device(l ^ 1, a)))
            elif a == nlat - 1:
                b_route.append((device(l, a), device(nlon - 1 - l, a)))
            else:
                b_route.append((device(l, a), device(l, a + (1 if a % 2 else -1))))
    both = ("lon", "lat")
    with jax.named_scope("halo"):
        ra_in = lax.ppermute(ra, both, a_route)
        rb_in = lax.ppermute(rb, both, b_route)
        near_in = lax.ppermute(near, "lon", near_route)
        far_in = lax.ppermute(far, "lon", far_route)
    with jax.named_scope("inside"):
        *base, pin, p62, p1 = pl.pallas_call(
            main_kernel,
            in_specs=[VM] * 5,
            out_specs=[VM] * 7,
            out_shape=[vfield] * 4 + [pltpu.VMEM((NK, NI), F32)] * 3,
            scratch_shapes=[pltpu.VMEM((NJ, NI), F32)] * 7 + [
                pltpu.VMEM((NK * 16 + 16, NI), F32),
                pltpu.VMEM((NJ + 16, NI), F32),
                pltpu.VMEM((4, NJ, NI), F32),
                pltpu.VMEM((4, NJ + 8, NI), F32),
                pltpu.VMEM((NJ, NI), F32),
            ],
            compiler_params=params,
            cost_estimate=pl.CostEstimate(
                flops=40_000_000, bytes_accessed=13_000_000, transcendentals=0
            ),
        )(kmt, *held)
    base = [near_core(x) for x in base]
    rest = [near_core(x) for x in (pin, p62, p1, near, far, near_in, far_in, ra_in, rb_in)]
    with jax.named_scope("edges"):
        return tuple(
            x.reshape(NK, NJ, NI)
            for x in pl.pallas_call(
                fix_kernel,
                in_specs=[VM] * 18,
                out_specs=[ANY] * 4,
                out_shape=[field] * 4,
                scratch_shapes=[
                    pltpu.VMEM((4, NK * NJ, NI), F32),
                    pltpu.VMEM((2, 4, NK, NI), F32),
                    pltpu.SemaphoreType.DMA((CH, 4)),
                ],
                compiler_params=params,
                cost_estimate=pl.CostEstimate(
                    flops=4_000_000, bytes_accessed=7_000_000, transcendentals=0
                ),
            )(kmt, *held, *base, *rest)
        )


def solution(mesh):
    grid = P(None, "lat", "lon")
    return jax.shard_map(
        shards,
        mesh=mesh,
        in_specs=(grid,) * 4 + (P("lat", "lon"),),
        out_specs=(grid,) * 4,
        check_vma=False,
    )
```

```python
import math

import jax
import jax.numpy as jnp
from jax import lax
from jax.experimental import pallas as pl
from jax.experimental.pallas import tpu as pltpu
from jax.sharding import PartitionSpec as P

NK, NJ, NI = 48, 64, 128
JT = NJ // 8
NQ = NK // 3
CH = 4
CK = NK // CH
F32 = jnp.float32
VM = pl.BlockSpec(memory_space=pltpu.VMEM)
ANY = pl.BlockSpec(memory_space=pl.ANY)
LIMIT = 48 * 1024 * 1024


def lanes():
    return lax.broadcasted_iota(jnp.int32, (8, NI), 1)


def subs():
    return lax.broadcasted_iota(jnp.int32, (8, NI), 0)


def roll(x, shift, axis):
    return pltpu.roll(x, shift, axis)


def place(k, jt):
    return pl.ds(pl.multiple_of(k * NJ, NJ) + 8 * jt, 8)


def tile(ref, k, jt):
    return ref[place(k, jt), :]


def split_pairs(a, b, even):
    return jnp.where(even, a, roll(b, 1, 1)), jnp.where(even, roll(a, 127, 1), b)


def join_pairs(e, w, even):
    return jnp.where(even, e, roll(w, 1, 1)), jnp.where(even, roll(e, 127, 1), w)


def level_terms(k):
    h = 1.0 + k * (1.0 / NK)
    z = (k + 1.0) + k * (k + 1.0) * (0.5 / NK) - 0.5 * h
    return 0.5 * h * (-0.6 + 0.03 * z), -0.05 * h, 0.4 * h


def packed_latitude():
    row = lax.axis_index("lat") * NJ + (lanes() & 7) * 8 + subs()
    total = NJ * lax.axis_size("lat")
    phi = (-75.0 + 150.0 * (row.astype(F32) + 0.5) / total) * (math.pi / 180.0)
    return 1.0 / jnp.cos(phi), 1.5 * jnp.sin(phi)


def pack_kernel(kmt, u, v, t, s, uo, vo, to, so, near, far, ra, rb, sem):
    copies = [
        [
            pltpu.make_async_copy(
                src.at[pl.ds(c * CK * NJ, CK * NJ)],
                dst.at[pl.ds(c * CK * NJ, CK * NJ)],
                sem.at[c, f],
            )
            for f, (src, dst) in enumerate(((u, uo), (v, vo), (t, to), (s, so)))
        ]
        for c in range(CH)
    ]
    for group in copies:
        for copy in group:
            copy.start()
    lon, lat = lax.axis_index("lon"), lax.axis_index("lat")
    lon_even, lat_even = lon % 2 == 0, lat % 2 == 0
    lane = lanes()
    even = (lane & 1) == 0
    spot = [(lane >> 1) == 60 + jh for jh in range(4)]
    outs = (uo, vo, to, so)

    def put(acc, tiles):
        for jh in range(4):
            acc = jnp.where(spot[jh], roll(tiles[jh], 121 + 2 * jh, 1), acc)
        return acc

    kf = [kmt[8 * jt : 8 * jt + 8, :].astype(F32) for jt in range(JT)]
    inner = [
        jnp.minimum(x, jnp.where(lane == 0, roll(x, 127, 1), roll(x, 1, 1))) for x in kf
    ]
    zero = jnp.zeros((8, NI), F32)
    for at, tiles in ((96, kf), (104, inner)):
        e, w = split_pairs(put(zero, tiles[0::2]), put(zero, tiles[1::2]), even)
        for shift in (8, 16, 32, 64):
            e = e + roll(e, shift, 1)
            w = w + roll(w, shift, 1)
        near[at : at + 8, :] = jnp.where(lon_even, e, w)
        far[at : at + 8, :] = jnp.where(lon_even, w, e)

    def step(q, carry):
        new = []
        for f in range(4):
            for i in range(3):
                k = q * 3 + i
                for half in range(2):
                    acc = roll(carry[f * 6 + i * 2 + half], 120, 1)
                    tiles = [tile(outs[f], k, jt) for jt in range(half, JT, 2)]
                    new.append(put(acc, tiles))
        return tuple(new)

    carry = (zero,) * 24
    for c in range(CH):
        for copy in copies[c]:
            copy.wait()
        carry = lax.fori_loop(c * NQ // CH, (c + 1) * NQ // CH, step, carry, unroll=4)
    for f in range(4):
        for i in range(3):
            e, w = split_pairs(carry[f * 6 + i * 2], carry[f * 6 + i * 2 + 1], even)
            at = (f * 3 + i) * 8
            near[at : at + 8, :] = jnp.where(lon_even, e, w)
            far[at : at + 8, :] = jnp.where(lon_even, w, e)

    fold = lat == lax.axis_size("lat") - 1
    order = jnp.where(fold, 127 - lane, lane)
    tops, bottoms = [], []
    for ref in outs:
        top = ref[pl.ds(NJ - 1, NK, stride=NJ), :]
        bottom = ref[pl.ds(0, NK, stride=NJ), :]
        for b in range(6):
            tops.append(top[8 * b : 8 * b + 8, :])
            bottoms.append(bottom[8 * b : 8 * b + 8, :])
    tops.append(jnp.broadcast_to(kf[JT - 1][7:8, :], (8, NI)))
    bottoms.append(jnp.broadcast_to(kf[0][0:1, :], (8, NI)))
    for n, (top, bottom) in enumerate(zip(tops, bottoms)):
        ra[8 * n : 8 * n + 8, :] = jnp.where(lat_even, top, bottom)
        rb[8 * n : 8 * n + 8, :] = jnp.take_along_axis(
            jnp.where(lat_even, bottom, top), order, axis=1, mode="promise_in_bounds"
        )


def main_kernel(
    kmt, u_ref, v_ref, t_ref, s_ref, ou, ov, ot, os, pin, p62, p1, ks, ke, kn, kew, kns, rs, fs, pins, press, flux, rise, inner
):
    kf = kmt[...].astype(F32)
    lane64 = lax.broadcasted_iota(jnp.int32, (NJ, NI), 1)
    row64 = lax.broadcasted_iota(jnp.int32, (NJ, NI), 0)
    k_e = jnp.minimum(kf, roll(kf, 127, 1))
    k_w = roll(kf, 1, 1)
    k_n = jnp.minimum(kf, roll(kf, NJ - 1, 0))
    k_s = roll(kf, 1, 0)
    ks[...] = kf
    ke[...] = jnp.where(lane64 == NI - 1, 0.0, k_e)
    kew[...] = jnp.where((lane64 == 0) | (lane64 == NI - 1), 0.0, jnp.minimum(k_e, k_w))
    kn[...] = jnp.where(row64 == NJ - 1, 0.0, k_n)
    kns[...] = jnp.where((row64 == 0) | (row64 == NJ - 1), 0.0, jnp.minimum(k_n, k_s))
    r, f = packed_latitude()
    for jt in range(JT):
        rs[8 * jt : 8 * jt + 8, :] = jnp.broadcast_to(0.025 * r[:, jt : jt + 1], (8, NI))
        fs[8 * jt : 8 * jt + 8, :] = jnp.broadcast_to(0.1 * f[:, jt : jt + 1], (8, NI))

    lane, row = lanes(), subs()
    first = lane == 0
    even = (lane & 1) == 0
    spot = [(lane >> 1) == 60 + jh for jh in range(4)]
    zero = jnp.zeros((8, NI), F32)

    def fixed(ref, jt):
        return ref[8 * jt : 8 * jt + 8, :]

    def after(ref, x, k, jt):
        if jt == JT - 1:
            return roll(x, 7, 0)
        return ref[pl.ds(pl.multiple_of(k * NJ, NJ) + 8 * jt + 1, 8), :]

    fields, outs = (u_ref, v_ref, t_ref, s_ref), (ou, ov, ot, os)

    def open_level(k, acc):
        kk = k.astype(F32)
        c1, c2, c3 = level_terms(kk)
        acc_new = []
        for jt in range(JT):
            q = [tile(ref, k, jt) for ref in fields]
            w = q[2] * (c1 + c2 * q[2]) + c3 * q[3]
            w = jnp.where(fixed(ks, jt) > kk, w, 0.0)
            p = acc[jt] + w
            press[8 + 8 * jt : 16 + 8 * jt, :] = p
            acc_new.append(p + w)
            qe = [x + roll(x, 127, 1) for x in q]
            flow = jnp.where(fixed(ke, jt) > kk, fixed(rs, jt), 0.0) * qe[0]
            for f in range(4):
                flux[f, 8 * jt : 8 * jt + 8, :] = flow * qe[f]
            qn = [x + after(ref, x, k, jt) for x, ref in zip(q, fields)]
            flow = jnp.where(fixed(kn, jt) > kk, 0.025, 0.0) * qn[1]
            for f in range(4):
                rise[f, 8 + 8 * jt : 16 + 8 * jt, :] = flow * qn[f]
        return tuple(acc_new)

    def close_level(k):
        kk = k.astype(F32)
        p62[pl.ds(k, 1), :] = press[8 + NJ - 2 : 8 + NJ - 1, :]
        p1[pl.ds(k, 1), :] = press[9:10, :]
        for jt in range(JT):
            q = [tile(ref, k, jt) for ref in fields]
            f01 = fixed(fs, jt)
            fe = [flux[f, 8 * jt : 8 * jt + 8, :] for f in range(4)]
            fn = [rise[f, 8 + 8 * jt : 16 + 8 * jt, :] for f in range(4)]
            fs_ = [rise[f, 7 + 8 * jt : 15 + 8 * jt, :] for f in range(4)]
            out = [
                x - (a - roll(a, 1, 1)) - (b - c) for x, a, b, c in zip(q, fe, fn, fs_)
            ]
            p = press[8 + 8 * jt : 16 + 8 * jt, :]
            pe, pw = roll(p, 127, 1), roll(p, 1, 1)
            inner[8 * jt : 8 * jt + 8, :] = jnp.where(first, pe, pw)
            slope = jnp.where(fixed(kew, jt) > kk, 2.0 * fixed(rs, jt), 0.0) * (pe - pw)
            out[0] = out[0] + (f01 * q[1] - slope)
            pn = press[9 + 8 * jt : 17 + 8 * jt, :]
            ps = press[7 + 8 * jt : 15 + 8 * jt, :]
            slope = jnp.where(fixed(kns, jt) > kk, 0.05, 0.0) * (pn - ps)
            out[1] = out[1] - (f01 * q[0] + slope)
            wet = fixed(ks, jt) > kk
            for ref, x in zip(outs, out):
                ref[place(k, jt), :] = jnp.where(wet, x, 0.0)

    def pack_inner(k):
        for half in range(2):
            edge = zero
            for jh in range(4):
                x = roll(fixed(inner, 2 * jh + half), 121 + 2 * jh, 1)
                edge = jnp.where(spot[jh], x, edge)
            pins[pl.ds(pl.multiple_of(k * 16, 16) + 8 * half, 8), :] = edge

    def level(k, acc):
        pack_inner(k)
        close_level(k)
        return open_level(jnp.minimum(k + 1, NK - 1), acc)

    inner[...] = jnp.zeros((NJ, NI), F32)
    press[0:8, :] = zero
    press[8 + NJ : 16 + NJ, :] = zero
    for f in range(4):
        rise[f, 0:8, :] = zero
    lax.fori_loop(0, NK, level, open_level(jnp.int32(0), (zero,) * JT), unroll=2)
    pack_inner(jnp.int32(NK))

    def gather(q, carry):
        at = pl.multiple_of(q * 48, 16) + 16
        return tuple(
            roll(x, 120, 1) + pins[pl.ds(at + 8 * n, 8), :] for n, x in enumerate(carry)
        )

    pairs = lax.fori_loop(0, NQ, gather, (zero,) * 6)
    for i in range(3):
        e, w = split_pairs(pairs[2 * i], pairs[2 * i + 1], even)
        pin[8 * i : 8 * i + 8, :] = e
        pin[24 + 8 * i : 32 + 8 * i, :] = w


def fix_kernel(
    kmt, u_ref, v_ref, t_ref, s_ref, bu, bv, bt, bs, pin, p62, p1,
    near, far, near_in, far_in, ra_in, rb_in, ou, ov, ot, os, buf, rows, sem,
):
    lon, lat = lax.axis_index("lon"), lax.axis_index("lat")
    lon_even, lat_even = lon % 2 == 0, lat % 2 == 0
    is_top, is_bottom = lat == lax.axis_size("lat") - 1, lat == 0
    lane, row = lanes(), subs()
    even = (lane & 1) == 0
    fields = (u_ref, v_ref, t_ref, s_ref)

    level48 = lax.broadcasted_iota(jnp.int32, (NK, NI), 0).astype(F32)
    row48 = lax.broadcasted_iota(jnp.int32, (NK, NI), 0)
    c1, c2, c3 = level_terms(level48)
    sign = jnp.where(is_top, -1.0, 1.0)
    for side in range(2):
        own_row, next_row = (NJ - 1, NJ - 2) if side == 0 else (0, 1)
        use_a = lat_even if side == 0 else jnp.logical_not(lat_even)
        halo = [
            jnp.where(use_a, ra_in[NK * f : NK * f + NK, :], rb_in[NK * f : NK * f + NK, :])
            for f in range(4)
        ]
        k_halo = jnp.where(use_a, ra_in[4 * NK : 4 * NK + 1, :], rb_in[4 * NK : 4 * NK + 1, :])
        if side == 0:
            halo[0], halo[1] = halo[0] * sign, halo[1] * sign
        else:
            k_halo = jnp.where(is_bottom, 0.0, k_halo)
        own = [
            ref[pl.ds(own_row, NK, stride=NJ), :] for ref in fields
        ]
        k_own = kmt[own_row : own_row + 1, :].astype(F32)
        k_next = kmt[next_row : next_row + 1, :].astype(F32)
        k_face = jnp.minimum(k_own, k_halo)
        w = halo[2] * (c1 + c2 * halo[2]) + c3 * halo[3]
        w = jnp.where(level48 < k_halo, w, 0.0)
        total = w + w
        shift = 1
        while shift < NK:
            total = total + jnp.where(row48 >= shift, roll(total, shift, 0), 0.0)
            shift *= 2
        press = total - w
        flow = jnp.where(level48 < k_face, 0.025, 0.0) * (own[1] + halo[1])
        if side == 0:
            flow = -flow
        slope = press - p62[...] if side == 0 else p1[...] - press
        slope = jnp.where(level48 < jnp.minimum(k_face, k_next), 0.05, 0.0) * slope
        for f in range(4):
            add = flow * (own[f] + halo[f])
            if f == 1:
                add = add - slope
            rows[side, f, :, :] = add

    r, _ = packed_latitude()
    r25 = 0.025 * r
    level_of = [((lane >> 3) * 3 + i).astype(F32) for i in range(3)]
    terms = [level_terms(x) for x in level_of]
    sides = []
    for side in range(2):
        use_near = lon_even if side == 0 else jnp.logical_not(lon_even)

        def block(a, b, at):
            return jnp.where(use_near, a[at : at + 8, :], b[at : at + 8, :])

        k_own, k_in = block(near, far, 96), block(near, far, 104)
        k_halo = block(near_in, far_in, 96)
        k_face = jnp.minimum(k_own, k_halo)
        k_three = jnp.minimum(k_in, k_halo)
        own = [[block(near, far, (f * 3 + i) * 8) for i in range(3)] for f in range(4)]
        halo = [[block(near_in, far_in, (f * 3 + i) * 8) for i in range(3)] for f in range(4)]
        ws = []
        for i in range(3):
            c1, c2, c3 = terms[i]
            w = halo[2][i] * (c1 + c2 * halo[2][i]) + c3 * halo[3][i]
            ws.append(jnp.where(level_of[i] < k_halo, w, 0.0))
        group = 2.0 * (ws[0] + ws[1] + ws[2])
        total = group
        for shift in (8, 16, 32, 64):
            total = total + jnp.where(lane >= shift, roll(total, shift, 1), 0.0)
        above = jnp.where(lane >= 8, roll(total, 8, 1), 0.0)
        corr = [[None] * 3 for _ in range(4)]
        for i in range(3):
            press = above + ws[i]
            above = press + ws[i]
            flow = jnp.where(level_of[i] < k_face, r25, 0.0) * (own[0][i] + halo[0][i])
            inner = pin[24 * side + 8 * i : 24 * side + 8 * i + 8, :]
            slope = press - inner if side == 0 else inner - press
            slope = jnp.where(level_of[i] < k_three, 2.0 * r25, 0.0) * slope
            if side == 0:
                flow = -flow
            for f in range(4):
                corr[f][i] = flow * (own[f][i] + halo[f][i])
            corr[0][i] = corr[0][i] - slope
        sides.append(corr)
    packs = []
    for f in range(4):
        for i in range(3):
            packs += list(join_pairs(sides[0][f][i], sides[1][f][i], even))

    border = (lane == 0) | (lane == NI - 1)
    last_row, first_row = row == 7, row == 0
    bases, outs = (bu, bv, bt, bs), (ou, ov, ot, os)

    def step(q, carry):
        new = []
        for f in range(4):
            for i in range(3):
                k = q * 3 + i
                for half in range(2):
                    pack = carry[f * 6 + i * 2 + half]
                    for jh in range(4):
                        jt = 2 * jh + half
                        x = tile(bases[f], k, jt)
                        x = x + jnp.where(border, roll(pack, 127 - 2 * jh, 1), 0.0)
                        if jt == 0:
                            x = x + jnp.where(first_row, rows[1, f, pl.ds(k, 1), :], 0.0)
                        if jt == JT - 1:
                            x = x + jnp.where(last_row, rows[0, f, pl.ds(k, 1), :], 0.0)
                        buf[f, place(k, jt), :] = x
                    new.append(roll(pack, 120, 1))
        return tuple(new)

    carry = tuple(packs)
    copies = []
    for c in range(CH):
        carry = lax.fori_loop(c * NQ // CH, (c + 1) * NQ // CH, step, carry, unroll=4)
        for f in range(4):
            copy = pltpu.make_async_copy(
                buf.at[f, pl.ds(c * CK * NJ, CK * NJ)],
                outs[f].at[pl.ds(c * CK * NJ, CK * NJ)],
                sem.at[c, f],
            )
            copy.start()
            copies.append(copy)
    for copy in copies:
        copy.wait()


def near_core(x):
    return pltpu.with_memory_space_constraint(x, pltpu.VMEM)


def shards(u, v, t, s, kmt):
    nlon, nlat = lax.axis_size("lon"), lax.axis_size("lat")
    u, v, t, s = (x.reshape(NK * NJ, NI) for x in (u, v, t, s))
    field = jax.ShapeDtypeStruct((NK * NJ, NI), F32)
    params = pltpu.CompilerParams(vmem_limit_bytes=LIMIT)
    vfield = pltpu.VMEM((NK * NJ, NI), F32)
    column = pltpu.VMEM((112, NI), F32)
    strip = pltpu.VMEM((200, NI), F32)
    with jax.named_scope("pack"):
        *held, near, far, ra, rb = pl.pallas_call(
            pack_kernel,
            in_specs=[VM] + [ANY] * 4,
            out_specs=[VM] * 8,
            out_shape=[vfield] * 4 + [column] * 2 + [strip] * 2,
            scratch_shapes=[pltpu.SemaphoreType.DMA((CH, 4))],
            compiler_params=params,
            cost_estimate=pl.CostEstimate(
                flops=4_000_000, bytes_accessed=7_000_000, transcendentals=0
            ),
        )(kmt, u, v, t, s)

    held = [near_core(x) for x in held]

    def device(lon, lat):
        return lon * nlat + lat

    near_route = [(l, l ^ 1) for l in range(nlon)]
    far_route = [(l, (l + (1 if l % 2 else -1)) % nlon) for l in range(nlon)]
    a_route, b_route = [], []
    for l in range(nlon):
        for a in range(nlat):
            a_route.append((device(l, a), device(l, a ^ 1)))
            if a == 0:
                b_route.append((device(l, a), device(l ^ 1, a)))
            elif a == nlat - 1:
                b_route.append((device(l, a), device(nlon - 1 - l, a)))
            else:
                b_route.append((device(l, a), device(l, a + (1 if a % 2 else -1))))
    both = ("lon", "lat")
    with jax.named_scope("halo"):
        ra_in = lax.ppermute(ra, both, a_route)
        rb_in = lax.ppermute(rb, both, b_route)
        near_in = lax.ppermute(near, "lon", near_route)
        far_in = lax.ppermute(far, "lon", far_route)
    with jax.named_scope("inside"):
        *base, pin, p62, p1 = pl.pallas_call(
            main_kernel,
            in_specs=[VM] * 5,
            out_specs=[VM] * 7,
            out_shape=[vfield] * 4 + [pltpu.VMEM((NK, NI), F32)] * 3,
            scratch_shapes=[pltpu.VMEM((NJ, NI), F32)] * 7 + [
                pltpu.VMEM((NK * 16 + 16, NI), F32),
                pltpu.VMEM((NJ + 16, NI), F32),
                pltpu.VMEM((4, NJ, NI), F32),
                pltpu.VMEM((4, NJ + 8, NI), F32),
                pltpu.VMEM((NJ, NI), F32),
            ],
            compiler_params=params,
            cost_estimate=pl.CostEstimate(
                flops=40_000_000, bytes_accessed=13_000_000, transcendentals=0
            ),
        )(kmt, *held)
    base = [near_core(x) for x in base]
    rest = [near_core(x) for x in (pin, p62, p1, near, far, near_in, far_in, ra_in, rb_in)]
    with jax.named_scope("edges"):
        return tuple(
            x.reshape(NK, NJ, NI)
            for x in pl.pallas_call(
                fix_kernel,
                in_specs=[VM] * 18,
                out_specs=[ANY] * 4,
                out_shape=[field] * 4,
                scratch_shapes=[
                    pltpu.VMEM((4, NK * NJ, NI), F32),
                    pltpu.VMEM((2, 4, NK, NI), F32),
                    pltpu.SemaphoreType.DMA((CH, 4)),
                ],
                compiler_params=params,
                cost_estimate=pl.CostEstimate(
                    flops=4_000_000, bytes_accessed=7_000_000, transcendentals=0
                ),
            )(kmt, *held, *base, *rest)
        )


def solution(mesh):
    grid = P(None, "lat", "lon")
    return jax.shard_map(
        shards,
        mesh=mesh,
        in_specs=(grid,) * 4 + (P("lat", "lon"),),
        out_specs=(grid,) * 4,
        check_vma=False,
    )
```
